512 devices in a mesh: grp: 4 (over x_hi, core), dev: 128 (over z, x_lo, y).
Axes of the slice: x: 4 (x_hi: 2, x_lo: 2; x = x_hi * 2 + x_lo), y: 8, z: 8, core: 2. Of those that a mesh axis runs over, the one named last changes fastest.
Arguments:
- velocity: float32 [1024, 3, 65536], P('dev', None, 'grp'), parts along dimension 2, may hold values from -6 to 6
- starts: int32 [3], replicated, may hold values from 0 to 512, as said below
- picks: int32 [16384], replicated, may hold values from 0 to 16383, each once
Outputs:
- spectra: float32 [9, 256, 65536], P(None, None, ('grp', 'dev')), parts along dimension 2
- plane_mean: float32 [12, 256], P('grp'), parts along dimension 0
The draws below stay inside these ranges and needn't reach their ends.
There are 4 independent parts, one for each index of `grp`. The reference program is written for one: setup_inputs(seed, part) draws one part's arguments, and reference() takes and returns one part's arrays. A program takes and returns all parts, laid end to end along the dimension named above; an argument that names none is the same for every part. Nothing has to cross between parts.
Inputs may be any that keep to these rules, and one draw needn't show every extreme that they name: The first window starts at 0, the last at 512; window w starts within 64 of w * 256. `picks`: every point appears exactly once.
All inputs are finite; a program needn't handle non-finite values.
Results may differ from the reference program's by a relative error of at most 0.0001.
Values sent between devices are 32-bit elements; how exact they have to be, the bound alone decides.
No kernel may reach another device: no remote copies, remote signals or barrier semaphores. Data moves between devices by JAX's collectives and lax.ppermute only.
A program may use at most 192 MiB of HBM per device.

```python
import math
import jax
import jax.numpy as jnp
from jax import lax

L = 512
HOP = 256
F = 256
W = 3
PD = 128
T_SIZE = 1024
P_SIZE = 16384
N_DEV = 128


def draw_starts(key, part):
    key = jax.random.fold_in(key, 11)
    index = jnp.arange(W, dtype=jnp.int32)
    jitter = jax.random.randint(key, (W,), -(HOP // 4), HOP // 4 + 1, dtype=jnp.int32)
    inner = (index > 0) & (index < W - 1)
    return (index * HOP + jnp.where(inner, jitter, 0)).astype(jnp.int32)


def block_levels(rng, dims, split, smallest, largest):
    gain, own = 1.0, jax.random.fold_in(rng, 6)
    for position, parts in split:
        heights = jnp.exp(jax.random.uniform(jax.random.fold_in(own, position), (parts,), jnp.float32, smallest / len(split), largest / len(split)))
        gain = gain * jnp.repeat(heights, dims[position] // parts).reshape([-1 if axis == position else 1 for axis in range(len(dims))])
    return gain


def noise(stream_key, shape, scale, bound, split=(), kind=jnp.bfloat16):
    array = scale * jax.random.normal(stream_key, shape, jnp.float32)
    if split:
        array = array * block_levels(stream_key, shape, split, -0.22, 0.18)
    return jnp.clip(array, -bound, bound).astype(kind)


def setup_inputs(seed: int = 0, part: int = 0) -> dict:
    key_of = jax.random.split(jax.random.key(seed), 4)
    own_keys = jax.random.split(jax.random.fold_in(key_of[3], part), 4)
    velocity = noise(own_keys[0], (T_SIZE, 3, P_SIZE), 1.0, 6.0, ((0, 128),), jnp.float32)
    starts = draw_starts(jax.random.fold_in(key_of[3], 71), part)
    picks = jax.random.permutation(key_of[2], PD * N_DEV).astype(jnp.int32)
    return dict(velocity=velocity, starts=starts, picks=picks)


def make_tables(length, bins):
    sample = jnp.arange(length, dtype=jnp.int32)
    freq = jnp.arange(bins, dtype=jnp.int32)
    phase = ((freq[:, None] * sample[None, :]) % length).astype(jnp.float32) * (2.0 * math.pi / length)
    basis = jnp.concatenate([jnp.cos(phase), -jnp.sin(phase)], axis=0)
    taper = 0.5 - 0.5 * jnp.cos(sample.astype(jnp.float32) * (2.0 * math.pi / length))
    return basis, taper


def block_spectra(series, starts, basis, taper, length, bins):
    count = starts.shape[0]
    width = series.shape[2]
    offsets = starts[:, None] + jnp.arange(length, dtype=jnp.int32)[None, :]
    frames = jnp.take(series, offsets.reshape(-1), axis=0).reshape(count, length, 3, width)
    centred = frames - jnp.mean(frames, axis=1, keepdims=True)
    tapered = centred * taper[None, :, None, None]
    matrix = jnp.transpose(tapered, (1, 0, 2, 3)).reshape(length, count * 3 * width)
    result = jnp.dot(basis, matrix, precision=lax.Precision.HIGHEST, preferred_element_type=jnp.float32)
    result = result.reshape(2, bins, count, 3, width)
    real_part, imag_part = result[0], result[1]
    scale = 1.0 / (jnp.sum(taper * taper) * count)
    rows = []
    for comp in range(3):
        rows.append(jnp.sum(real_part[:, :, comp] ** 2 + imag_part[:, :, comp] ** 2, axis=1) * scale)
    pairs = ((0, 1), (0, 2), (1, 2))
    for first, second in pairs:
        rows.append(jnp.sum(real_part[:, :, first] * real_part[:, :, second] + imag_part[:, :, first] * imag_part[:, :, second], axis=1) * scale)
    for first, second in pairs:
        rows.append(jnp.sum(real_part[:, :, first] * imag_part[:, :, second] - imag_part[:, :, first] * real_part[:, :, second], axis=1) * scale)
    return jnp.stack(rows, axis=0)


def reference(velocity, starts, picks):
    basis, taper = make_tables(L, F)
    blocks = picks.reshape(N_DEV, PD)

    def one_block(pick_block):
        series = jnp.take(velocity, pick_block, axis=2)
        return block_spectra(series, starts, basis, taper, L, F)

    stacked = lax.map(one_block, blocks)
    spectra = jnp.transpose(stacked, (1, 2, 0, 3)).reshape(9, F, N_DEV * PD)
    plane_mean = jnp.sum(spectra[:3], axis=2) / (N_DEV * PD)
    return spectra, plane_mean
```

```python
import functools

import jax
import jax.numpy as jnp
import ml_dtypes
import numpy as np
from jax import lax
from jax.experimental import pallas as pl
from jax.experimental.pallas import tpu as pltpu
from jax.sharding import Mesh, PartitionSpec as P

L = 512
F = 256
W = 3
LANES = 128
QUARTERS = 4
DEV = ("z", "xl", "y")


def split_bf16(table):
    high = table.astype(ml_dtypes.bfloat16)
    low = (table - high.astype(np.float64)).astype(ml_dtypes.bfloat16)
    return high, low


def make_tables():
    half = np.arange(L // 2)
    bins = np.arange(F // 2)
    bases = []
    for odd in (0, 1):
        phase = ((2 * bins[:, None] + odd) * half[None, :] % L) * (2.0 * np.pi / L)
        bases.append(np.concatenate([np.cos(phase), -np.sin(phase)], axis=0))
    high, low = split_bf16(np.stack(bases))
    turn = np.arange(L) * (2.0 * np.pi / L)
    turns = np.stack([np.cos(turn), np.sin(turn)]).astype(np.float32)
    turns = np.broadcast_to(turns[:, :, None], (2, L, LANES))
    taper = 0.5 - 0.5 * np.cos(turn)
    return high, low, np.ascontiguousarray(turns), float(1.0 / (np.sum(taper * taper) * W))


BASIS_HIGH, BASIS_LOW, TURNS, SCALE = make_tables()


def gather_kernel(
    picks_ref, x_ref, out_ref, picks, x, table, index, even, odd, out, sems, index_sems, x_sems, out_sems
):
    rows, points = x.shape
    blocks = out.shape[0]
    quarter = points // QUARTERS
    apart = LANES // QUARTERS
    pieces = x_sems.shape[0]
    width = quarter // pieces
    chunks = out_sems.shape[0]
    size = blocks // chunks
    together = even.shape[0]

    picks_copy = pltpu.make_async_copy(picks_ref, picks, sems.at[0])
    picks_copy.start()
    x_copies = []
    for piece in range(pieces):
        for q in range(QUARTERS):
            span = pl.ds(q * quarter + piece * width, width)
            x_copies.append(
                pltpu.make_async_copy(x_ref.at[:, span], x.at[:, span], x_sems.at[piece, q])
            )
    for copy in x_copies:
        copy.start()
    picks_copy.wait()
    index[...] = picks[...] % quarter

    def index_copy(slot, first):
        held = (even, odd)[slot]
        return pltpu.make_async_copy(index.at[pl.ds(first, together)], held, index_sems.at[slot])

    index_copy(0, 0).start()
    index_copy(1, together).start()

    pad = jnp.zeros((apart - rows, LANES), jnp.float32)
    for piece in range(pieces):
        for copy in x_copies[piece * QUARTERS : (piece + 1) * QUARTERS]:
            copy.wait()

        for block in range(width // LANES):
            start = piece * width + block * LANES
            parts = []
            for q in range(QUARTERS):
                parts += [x[:, q * quarter + start : q * quarter + start + LANES], pad]
            table[start : start + LANES, :] = jnp.concatenate(parts, axis=0).T

    point_rows = table.reshape(quarter, 1, LANES)
    row = lax.broadcasted_iota(jnp.int32, (8, LANES), 0)

    def pick(held, block):
        tiles = []
        for tile in range(LANES // 8):
            parts = [
                jnp.broadcast_to(point_rows[held[block, tile * 8 + j]], (8, LANES))
                for j in range(8)
            ]
            step = 1
            while len(parts) > 1:
                mask = (row & step) == 0
                parts = [jnp.where(mask, parts[i], parts[i + 1]) for i in range(0, len(parts), 2)]
                step *= 2
            tiles.append(parts[0])
        return jnp.concatenate(tiles, axis=0)

    def keep(block, turned):
        which = jnp.broadcast_to(picks[pl.ds(block, 1), :], (rows, LANES))
        value = turned[0:rows]
        for q in range(1, QUARTERS):
            part = turned[q * apart : q * apart + rows]
            value = jnp.where(which >= q * quarter, part, value)
        out[block] = value

    def batch(held, first, before):
        for i in range(together):
            picked = pick(held, i)
            keep(jnp.maximum(first + i - 1, 0), before.T)
            before = picked
        return before

    def chunk_copy(chunk):
        span = pl.ds(chunk * size, size)
        return pltpu.make_async_copy(out.at[span], out_ref.at[span], out_sems.at[chunk])

    def chunk_step(chunk, before):
        for slot, held in enumerate((even, odd)):
            first = chunk * size + slot * together
            index_copy(slot, first).wait()
            before = batch(held, first, before)

            @pl.when(chunk < chunks - 1)
            def _():
                index_copy(slot, first + size).start()

            if slot == 0:

                @pl.when(chunk > 0)
                def _():
                    chunk_copy(chunk - 1).start()

        return before

    last = lax.fori_loop(0, chunks, chunk_step, jnp.zeros((LANES, LANES), jnp.float32))
    keep(blocks - 1, last.T)
    chunk_copy(chunks - 1).start()

    def finish(chunk, carry):
        chunk_copy(chunk).wait()
        return carry

    lax.fori_loop(0, chunks, finish, 0)


def gather_points(picks, x):
    rows, points = x.shape
    blocks = points // LANES
    pieces = points // QUARTERS // 1024
    vmem = pltpu.VMEM
    return pl.pallas_call(
        gather_kernel,
        out_shape=jax.ShapeDtypeStruct((blocks, rows, LANES), jnp.float32),
        in_specs=[pl.BlockSpec(memory_space=pl.ANY)] * 2,
        out_specs=pl.BlockSpec(memory_space=pl.ANY),
        scratch_shapes=[
            vmem((blocks, LANES), jnp.int32),
            vmem((rows, points), jnp.float32),
            vmem((points // QUARTERS, LANES), jnp.float32),
            vmem((blocks, LANES), jnp.int32),
            pltpu.SMEM((8, LANES), jnp.int32),
            pltpu.SMEM((8, LANES), jnp.int32),
            vmem((blocks, rows, LANES), jnp.float32),
            pltpu.SemaphoreType.DMA((1,)),
            pltpu.SemaphoreType.DMA((2,)),
            pltpu.SemaphoreType.DMA((pieces, QUARTERS)),
            pltpu.SemaphoreType.DMA((8,)),
        ],
        compiler_params=pltpu.CompilerParams(vmem_limit_bytes=58 * 2**20),
        name="gather_points",
    )(picks.reshape(blocks, LANES), x)


def transforms_kernel(points, starts_ref, x_ref, high_ref, low_ref, turns_ref, res_ref, own_ref, power_ref):
    half = L // 2
    sample = lax.broadcasted_iota(jnp.int32, (L, LANES), 0)
    for w in range(W):
        start = starts_ref[w]
        turn = lax.rem(start, L)
        cos_start = turns_ref[0, pl.ds(turn, 1), :]
        sin_start = turns_ref[1, pl.ds(turn, 1), :]
        taper = 0.5 - 0.5 * (turns_ref[0] * cos_start + turns_ref[1] * sin_start)
        late = sample >= start
        terms = [[], []]
        for comp in range(3):
            series = x_ref[:, comp * 8 : comp * 8 + 8, :].reshape(2 * L, LANES)
            frame = jnp.where(late, series[0:L], series[L : 2 * L])
            centred = frame - jnp.sum(frame, axis=0, keepdims=True) * (1.0 / L)
            tapered = centred * taper
            terms[0].append(tapered[0:half] + tapered[half:L])
            terms[1].append(tapered[0:half] - tapered[half:L])
        for odd in (0, 1):
            term = jnp.concatenate(terms[odd], axis=1)
            high = term.astype(jnp.bfloat16)
            low = (term - high.astype(jnp.float32)).astype(jnp.bfloat16)
            dot = functools.partial(jnp.dot, preferred_element_type=jnp.float32)
            res_ref[w, odd] = (
                dot(high_ref[odd], high) + dot(high_ref[odd], low) + dot(low_ref[odd], high)
            )

    for odd in (0, 1):
        power = jnp.zeros((F // 2, 3 * LANES), jnp.float32)
        for w in range(W):
            real, imag = res_ref[w, odd, 0 : F // 2, :], res_ref[w, odd, F // 2 : F, :]
            power += real * real + imag * imag
        for comp in range(3):
            span = slice(comp * LANES, (comp + 1) * LANES)
            power_ref[comp, pl.ds(odd, F // 2, stride=2), :] = power[:, span]
    ones = jnp.ones((8, LANES), jnp.float32)
    for comp in range(3):
        sums = lax.dot_general(
            ones,
            power_ref[comp],
            (((1,), (1,)), ((), ())),
            precision=lax.Precision.HIGHEST,
            preferred_element_type=jnp.float32,
        )
        own_ref[comp : comp + 1, :] = sums[0:1] * (SCALE / points)


def rows_kernel(res_ref, spectra_ref, out_ref, out_sems):
    rows = 8
    bins = F // 2

    def combine(step, carry):
        first = pl.multiple_of(step * rows, rows)
        for odd in (0, 1):
            totals = [None] * 9
            for w in range(W):
                real = [
                    res_ref[w, odd, pl.ds(first, rows), comp * LANES : (comp + 1) * LANES]
                    for comp in range(3)
                ]
                imag = [
                    res_ref[w, odd, pl.ds(bins + first, rows), comp * LANES : (comp + 1) * LANES]
                    for comp in range(3)
                ]
                terms = [real[c] * real[c] + imag[c] * imag[c] for c in range(3)]
                pairs = ((0, 1), (0, 2), (1, 2))
                terms += [real[i] * real[j] + imag[i] * imag[j] for i, j in pairs]
                terms += [real[i] * imag[j] - imag[i] * real[j] for i, j in pairs]
                totals = [b if a is None else a + b for a, b in zip(totals, terms)]
            for row in range(9):
                out_ref[row, pl.ds(2 * first + odd, rows, stride=2), :] = totals[row] * SCALE
        return carry

    pieces = out_sems.shape[0]
    copies = []
    for piece in range(pieces):
        steps = bins // rows // pieces
        lax.fori_loop(piece * steps, (piece + 1) * steps, combine, 0)
        span = pl.ds(piece * (F // pieces), F // pieces)
        copies.append(
            pltpu.make_async_copy(out_ref.at[:, span], spectra_ref.at[:, span], out_sems.at[piece])
        )
        copies[piece].start()
    for copy in copies:
        copy.wait()


def window_transforms(starts, arrived, points):
    vmem = pl.BlockSpec(memory_space=pltpu.VMEM)
    return pl.pallas_call(
        functools.partial(transforms_kernel, points),
        out_shape=(
            jax.ShapeDtypeStruct((W, 2, F, 3 * LANES), jnp.float32),
            jax.ShapeDtypeStruct((3, F), jnp.float32),
        ),
        in_specs=[pl.BlockSpec(memory_space=pltpu.SMEM)] + [vmem] * 4,
        out_specs=(vmem, vmem),
        scratch_shapes=[pltpu.VMEM((3, F, LANES), jnp.float32)],
        compiler_params=pltpu.CompilerParams(vmem_limit_bytes=28 * 2**20),
        name="window_transforms",
    )(starts, arrived, jnp.asarray(BASIS_HIGH), jnp.asarray(BASIS_LOW), jnp.asarray(TURNS))


def spectra_rows(transforms):
    return pl.pallas_call(
        rows_kernel,
        out_shape=jax.ShapeDtypeStruct((9, F, LANES), jnp.float32),
        in_specs=[pl.BlockSpec(memory_space=pltpu.VMEM)],
        out_specs=pl.BlockSpec(memory_space=pl.ANY),
        scratch_shapes=[
            pltpu.VMEM((9, F, LANES), jnp.float32),
            pltpu.SemaphoreType.DMA((4,)),
        ],
        compiler_params=pltpu.CompilerParams(vmem_limit_bytes=28 * 2**20),
        cost_estimate=pl.CostEstimate(flops=0, bytes_accessed=12 * 2**20, transcendentals=0),
        name="spectra_rows",
    )(transforms)


def sum_over(value, axes):
    count = lax.axis_size(axes)
    copies = jnp.broadcast_to(value[None], (count, *value.shape))
    return jnp.sum(lax.all_to_all(copies, axes, 0, 0, tiled=True), axis=0)


def on_device(velocity, starts, picks):
    times, comps, points = velocity.shape
    x = jnp.transpose(velocity, (1, 0, 2)).reshape(comps * times, points)
    chosen = gather_points(picks, x)
    arrived = lax.all_to_all(chosen, DEV, 0, 0, tiled=True)
    transforms, own = window_transforms(starts, arrived, points)
    spectra = spectra_rows(transforms)
    return (spectra, sum_over(sum_over(own, ("xl", "y")), "z"))


def solution(mesh):
    fine = Mesh(mesh.devices.reshape(4, 8, 2, 8), ("grp", *DEV))
    return jax.shard_map(
        on_device,
        mesh=fine,
        in_specs=(P(DEV, None, "grp"), P(), P()),
        out_specs=(P(None, None, ("grp", *DEV)), P("grp", None)),
        check_vma=False,
    )
```

```python
import functools

import jax
import jax.numpy as jnp
import ml_dtypes
import numpy as np
from jax import lax
from jax.experimental import pallas as pl
from jax.experimental.pallas import tpu as pltpu
from jax.sharding import Mesh, PartitionSpec as P

L = 512
F = 256
W = 3
LANES = 128
QUARTERS = 4
DEV = ("z", "xl", "y")


def make_tables():
    half = np.arange(L // 2)
    bins = np.arange(F // 2)
    bases = []
    for odd in (0, 1):
        phase = ((2 * bins[:, None] + odd) * half[None, :] % L) * (2.0 * np.pi / L)
        basis = np.concatenate([np.cos(phase), -np.sin(phase)], axis=0)
        high = basis.astype(ml_dtypes.bfloat16)
        low = (basis - high.astype(np.float64)).astype(ml_dtypes.bfloat16)
        bases.append(np.concatenate([high, high, low], axis=1))
    turn = np.arange(L) * (2.0 * np.pi / L)
    taper = 0.5 - 0.5 * np.cos(turn)
    turns = np.stack([np.cos(turn), np.sin(turn), taper]).astype(np.float32)
    turns = np.ascontiguousarray(np.broadcast_to(turns[:, :, None], (3, L, LANES)))
    return np.stack(bases), turns, float(1.0 / (np.sum(taper * taper) * W))


BASES, TURNS, SCALE = make_tables()


def gather_kernel(
    picks_ref, x_ref, out_ref, picks, x, table, index, which, even, odd, out, sems, index_sems, x_sems, out_sems
):
    rows, points = x.shape
    blocks = out.shape[0]
    quarter = points // QUARTERS
    apart = LANES // QUARTERS
    pieces = x_sems.shape[0]
    width = quarter // pieces
    chunks = out_sems.shape[0]
    size = blocks // chunks
    together = even.shape[0]

    picks_copy = pltpu.make_async_copy(picks_ref, picks, sems.at[0])
    picks_copy.start()
    x_copies = []
    for piece in range(pieces):
        span = pl.ds(piece * width * QUARTERS, width * QUARTERS)
        x_copies.append(pltpu.make_async_copy(x_ref.at[:, span], x.at[:, span], x_sems.at[piece]))
        x_copies[piece].start()
    picks_copy.wait()
    source = picks[...] // LANES
    index[...] = source // QUARTERS * LANES + picks[...] % LANES
    which[...] = source % QUARTERS

    def index_copy(slot, first):
        held = (even, odd)[slot]
        return pltpu.make_async_copy(index.at[pl.ds(first, together)], held, index_sems.at[slot])

    index_copy(0, 0).start()
    index_copy(1, together).start()

    pad = jnp.zeros((apart - rows, LANES), jnp.float32)
    for copy in x_copies:
        copy.wait()
    for block in range(quarter // LANES):
        parts = []
        for q in range(QUARTERS):
            start = (block * QUARTERS + q) * LANES
            parts += [x[:, start : start + LANES], pad]
        table[block * LANES : (block + 1) * LANES, :] = jnp.concatenate(parts, axis=0).T

    point_rows = table.reshape(quarter, 1, LANES)
    row = lax.broadcasted_iota(jnp.int32, (8, LANES), 0)

    def pick(held, block):
        tiles = []
        for tile in range(LANES // 8):
            parts = [
                jnp.broadcast_to(point_rows[held[block, tile * 8 + j]], (8, LANES))
                for j in range(8)
            ]
            step = 1
            while len(parts) > 1:
                mask = (row & step) == 0
                parts = [jnp.where(mask, parts[i], parts[i + 1]) for i in range(0, len(parts), 2)]
                step *= 2
            tiles.append(parts[0])
        return jnp.concatenate(tiles, axis=0)

    def keep(block, turned):
        chosen = jnp.broadcast_to(which[pl.ds(block, 1), :], (rows, LANES))
        value = turned[0:rows]
        for q in range(1, QUARTERS):
            part = turned[q * apart : q * apart + rows]
            value = jnp.where(chosen == q, part, value)
        out[block] = value

    def batch(held, first, before):
        for i in range(together):
            picked = pick(held, i)
            keep(jnp.maximum(first + i - 1, 0), before.T)
            before = picked
        return before

    def chunk_copy(chunk):
        span = pl.ds(chunk * size, size)
        return pltpu.make_async_copy(out.at[span], out_ref.at[span], out_sems.at[chunk])

    def chunk_step(chunk, before):
        for slot, held in enumerate((even, odd)):
            first = chunk * size + slot * together
            index_copy(slot, first).wait()
            before = batch(held, first, before)

            @pl.when(chunk < chunks - 1)
            def _():
                index_copy(slot, first + size).start()

            if slot == 0:

                @pl.when(chunk > 0)
                def _():
                    chunk_copy(chunk - 1).start()

        return before

    last = lax.fori_loop(0, chunks, chunk_step, jnp.zeros((LANES, LANES), jnp.float32))
    keep(blocks - 1, last.T)
    chunk_copy(chunks - 1).start()

    def finish(chunk, carry):
        chunk_copy(chunk).wait()
        return carry

    lax.fori_loop(0, chunks, finish, 0)


def gather_points(picks, x):
    rows, points = x.shape
    blocks = points // LANES
    pieces = points // QUARTERS // 1024
    vmem = pltpu.VMEM
    return pl.pallas_call(
        gather_kernel,
        out_shape=jax.ShapeDtypeStruct((blocks, rows, LANES), jnp.float32),
        in_specs=[pl.BlockSpec(memory_space=pl.ANY)] * 2,
        out_specs=pl.BlockSpec(memory_space=pl.ANY),
        scratch_shapes=[
            vmem((blocks, LANES), jnp.int32),
            vmem((rows, points), jnp.float32),
            vmem((points // QUARTERS, LANES), jnp.float32),
            vmem((blocks, LANES), jnp.int32),
            vmem((blocks, LANES), jnp.int32),
            pltpu.SMEM((16, LANES), jnp.int32),
            pltpu.SMEM((16, LANES), jnp.int32),
            vmem((blocks, rows, LANES), jnp.float32),
            pltpu.SemaphoreType.DMA((1,)),
            pltpu.SemaphoreType.DMA((2,)),
            pltpu.SemaphoreType.DMA((pieces,)),
            pltpu.SemaphoreType.DMA((4,)),
        ],
        compiler_params=pltpu.CompilerParams(vmem_limit_bytes=58 * 2**20),
        name="gather_points",
    )(picks.reshape(blocks, LANES), x)


def transforms_kernel(points, starts_ref, x_ref, bases_ref, turns_ref, res_ref, own_ref, power_ref):
    half = L // 2
    sample = lax.broadcasted_iota(jnp.int32, (L, LANES), 0)
    for w in range(W):
        if 0 < w < W - 1:
            start = starts_ref[w]
            turn = lax.rem(start, L)
            cos_start = turns_ref[0, pl.ds(turn, 1), :]
            sin_start = turns_ref[1, pl.ds(turn, 1), :]
            taper = 0.5 - 0.5 * (turns_ref[0] * cos_start + turns_ref[1] * sin_start)
            late = sample >= start
        else:
            taper = turns_ref[2]
        terms = [[], []]
        for comp in range(3):
            series = x_ref[:, comp * 8 : comp * 8 + 8, :].reshape(2 * L, LANES)
            if w == 0:
                frame = series[0:L]
            elif w == W - 1:
                frame = series[L : 2 * L]
            else:
                frame = jnp.where(late, series[0:L], series[L : 2 * L])
            centred = frame - jnp.sum(frame, axis=0, keepdims=True) * (1.0 / L)
            tapered = centred * taper
            terms[0].append(tapered[0:half] + tapered[half:L])
            terms[1].append(tapered[0:half] - tapered[half:L])
        for odd in (0, 1):
            term = jnp.concatenate(terms[odd], axis=1)
            high = term.astype(jnp.bfloat16)
            low = (term - high.astype(jnp.float32)).astype(jnp.bfloat16)
            res_ref[w, odd] = jnp.dot(
                bases_ref[odd],
                jnp.concatenate([high, low, high], axis=0),
                preferred_element_type=jnp.float32,
            )

    for odd in (0, 1):
        power = jnp.zeros((F // 2, 3 * LANES), jnp.float32)
        for w in range(W):
            real, imag = res_ref[w, odd, 0 : F // 2, :], res_ref[w, odd, F // 2 : F, :]
            power += real * real + imag * imag
        for comp in range(3):
            span = slice(comp * LANES, (comp + 1) * LANES)
            power_ref[comp, pl.ds(odd, F // 2, stride=2), :] = power[:, span]
    ones = jnp.ones((16, LANES), jnp.bfloat16)
    for comp in range(3):
        power = power_ref[comp]
        high = power.astype(jnp.bfloat16)
        low = (power - high.astype(jnp.float32)).astype(jnp.bfloat16)
        sums = [
            lax.dot_general(
                ones, term, (((1,), (1,)), ((), ())), preferred_element_type=jnp.float32
            )[0:1]
            for term in (high, low)
        ]
        share = (sums[0] + sums[1]) * (SCALE / points)
        for copy in range(own_ref.shape[0]):
            own_ref[copy, :, comp * F : (comp + 1) * F] = share


def rows_kernel(res_ref, spectra_ref, out_ref, out_sems):
    rows = 8
    bins = F // 2

    def combine(step, carry):
        first = pl.multiple_of(step * rows, rows)
        for odd in (0, 1):
            totals = [None] * 9
            for w in range(W):
                real = [
                    res_ref[w, odd, pl.ds(first, rows), comp * LANES : (comp + 1) * LANES]
                    for comp in range(3)
                ]
                imag = [
                    res_ref[w, odd, pl.ds(bins + first, rows), comp * LANES : (comp + 1) * LANES]
                    for comp in range(3)
                ]
                terms = [real[c] * real[c] + imag[c] * imag[c] for c in range(3)]
                pairs = ((0, 1), (0, 2), (1, 2))
                terms += [real[i] * real[j] + imag[i] * imag[j] for i, j in pairs]
                terms += [real[i] * imag[j] - imag[i] * real[j] for i, j in pairs]
                totals = [b if a is None else a + b for a, b in zip(totals, terms)]
            for row in range(9):
                out_ref[row, pl.ds(2 * first + odd, rows, stride=2), :] = totals[row] * SCALE
        return carry

    pieces = out_sems.shape[0]
    copies = []
    for piece in range(pieces):
        steps = bins // rows // pieces
        lax.fori_loop(piece * steps, (piece + 1) * steps, combine, 0)
        span = pl.ds(piece * (F // pieces), F // pieces)
        copies.append(
            pltpu.make_async_copy(out_ref.at[:, span], spectra_ref.at[:, span], out_sems.at[piece])
        )
        copies[piece].start()
    for copy in copies:
        copy.wait()


def window_transforms(starts, arrived, points, copies):
    vmem = pl.BlockSpec(memory_space=pltpu.VMEM)
    return pl.pallas_call(
        functools.partial(transforms_kernel, points),
        out_shape=(
            jax.ShapeDtypeStruct((W, 2, F, 3 * LANES), jnp.float32),
            jax.ShapeDtypeStruct((copies, 1, 3 * F), jnp.float32),
        ),
        in_specs=[pl.BlockSpec(memory_space=pltpu.SMEM)] + [vmem] * 3,
        out_specs=(vmem, vmem),
        scratch_shapes=[pltpu.VMEM((3, F, LANES), jnp.float32)],
        compiler_params=pltpu.CompilerParams(vmem_limit_bytes=28 * 2**20),
        name="window_transforms",
    )(starts, arrived, jnp.asarray(BASES), jnp.asarray(TURNS))


def spectra_rows(transforms):
    return pl.pallas_call(
        rows_kernel,
        out_shape=jax.ShapeDtypeStruct((9, F, LANES), jnp.float32),
        in_specs=[pl.BlockSpec(memory_space=pltpu.VMEM)],
        out_specs=pl.BlockSpec(memory_space=pl.ANY),
        scratch_shapes=[
            pltpu.VMEM((9, F, LANES), jnp.float32),
            pltpu.SemaphoreType.DMA((4,)),
        ],
        compiler_params=pltpu.CompilerParams(vmem_limit_bytes=28 * 2**20),
        cost_estimate=pl.CostEstimate(flops=0, bytes_accessed=12 * 2**20, transcendentals=0),
        name="spectra_rows",
    )(transforms)


def on_device(velocity, starts, picks):
    times, comps, points = velocity.shape
    x = jnp.transpose(velocity, (1, 0, 2)).reshape(comps * times, points)
    chosen = gather_points(picks, x)
    arrived = lax.all_to_all(chosen, DEV, 0, 0, tiled=True)
    plane = ("z", "y")
    transforms, copies = window_transforms(starts, arrived, points, lax.axis_size(plane))
    spectra = spectra_rows(transforms)
    total = jnp.sum(lax.all_to_all(copies, plane, 0, 0, tiled=True), axis=0)
    return (spectra, lax.psum(total.reshape(3, F), "xl"))


def solution(mesh):
    fine = Mesh(mesh.devices.reshape(4, 8, 2, 8), ("grp", *DEV))
    return jax.shard_map(
        on_device,
        mesh=fine,
        in_specs=(P(DEV, None, "grp"), P(), P()),
        out_specs=(P(None, None, ("grp", *DEV)), P("grp", None)),
        check_vma=False,
    )
```

```python
import functools

import jax
import jax.numpy as jnp
import ml_dtypes
import numpy as np
from jax import lax
from jax.experimental import pallas as pl
from jax.experimental.pallas import tpu as pltpu
from jax.sharding import Mesh, PartitionSpec as P

L = 512
F = 256
W = 3
LANES = 128
QUARTERS = 4
DEV = ("z", "xl", "y")


def make_tables():
    half = np.arange(L // 2)
    bins = np.arange(F // 2)
    bases = []
    for odd in (0, 1):
        phase = ((2 * bins[:, None] + odd) * half[None, :] % L) * (2.0 * np.pi / L)
        basis = np.concatenate([np.cos(phase), -np.sin(phase)], axis=0)
        high = basis.astype(ml_dtypes.bfloat16)
        low = (basis - high.astype(np.float64)).astype(ml_dtypes.bfloat16)
        bases.append(np.concatenate([high, high, low], axis=1))
    turn = np.arange(L) * (2.0 * np.pi / L)
    taper = 0.5 - 0.5 * np.cos(turn)
    turns = np.stack([np.cos(turn), np.sin(turn), taper]).astype(np.float32)
    turns = np.ascontiguousarray(np.broadcast_to(turns[:, :, None], (3, L, LANES)))
    return np.stack(bases), turns, float(1.0 / (np.sum(taper * taper) * W))


BASES, TURNS, SCALE = make_tables()


def gather_kernel(
    picks_ref, x_ref, out_ref, picks, x, table, index, which, even, odd, out, sems, index_sems, x_sems, out_sems
):
    rows, points = x.shape
    blocks = out.shape[0]
    quarter = points // QUARTERS
    apart = LANES // QUARTERS
    pieces = x_sems.shape[0]
    width = quarter // pieces
    chunks = out_sems.shape[0]
    size = blocks // chunks
    together = even.shape[0]

    picks_copy = pltpu.make_async_copy(picks_ref, picks, sems.at[0])
    picks_copy.start()
    x_copies = []
    for piece in range(pieces):
        span = pl.ds(piece * width * QUARTERS, width * QUARTERS)
        x_copies.append(pltpu.make_async_copy(x_ref.at[:, span], x.at[:, span], x_sems.at[piece]))
        x_copies[piece].start()
    picks_copy.wait()
    source = picks[...] // LANES
    index[...] = source // QUARTERS * LANES + picks[...] % LANES
    which[...] = source % QUARTERS

    def index_copy(slot, first):
        held = (even, odd)[slot]
        return pltpu.make_async_copy(index.at[pl.ds(first, together)], held, index_sems.at[slot])

    index_copy(0, 0).start()
    index_copy(1, together).start()

    pad = jnp.zeros((apart - rows, LANES), jnp.float32)
    for copy in x_copies:
        copy.wait()
    for block in range(quarter // LANES):
        parts = []
        for q in range(QUARTERS):
            start = (block * QUARTERS + q) * LANES
            parts += [x[:, start : start + LANES], pad]
        table[block * LANES : (block + 1) * LANES, :] = jnp.concatenate(parts, axis=0).T

    point_rows = table.reshape(quarter, 1, LANES)
    row = lax.broadcasted_iota(jnp.int32, (8, LANES), 0)

    def pick(held, block):
        tiles = []
        for tile in range(LANES // 8):
            parts = [
                jnp.broadcast_to(point_rows[held[block, tile * 8 + j]], (8, LANES))
                for j in range(8)
            ]
            step = 1
            while len(parts) > 1:
                mask = (row & step) == 0
                parts = [jnp.where(mask, parts[i], parts[i + 1]) for i in range(0, len(parts), 2)]
                step *= 2
            tiles.append(parts[0])
        return jnp.concatenate(tiles, axis=0)

    def keep(block, turned):
        chosen = jnp.broadcast_to(which[pl.ds(block, 1), :], (rows, LANES))
        value = turned[0:rows]
        for q in range(1, QUARTERS):
            part = turned[q * apart : q * apart + rows]
            value = jnp.where(chosen == q, part, value)
        out[block] = value

    def batch(held, first, before):
        for i in range(together):
            picked = pick(held, i)
            keep(jnp.maximum(first + i - 1, 0), before.T)
            before = picked
        return before

    def chunk_copy(chunk):
        span = pl.ds(chunk * size, size)
        return pltpu.make_async_copy(out.at[span], out_ref.at[span], out_sems.at[chunk])

    def chunk_step(chunk, before):
        for slot, held in enumerate((even, odd)):
            first = chunk * size + slot * together
            index_copy(slot, first).wait()
            before = batch(held, first, before)

            @pl.when(chunk < chunks - 1)
            def _():
                index_copy(slot, first + size).start()

            if slot == 0:

                @pl.when(chunk > 0)
                def _():
                    chunk_copy(chunk - 1).start()

        return before

    last = lax.fori_loop(0, chunks, chunk_step, jnp.zeros((LANES, LANES), jnp.float32))
    keep(blocks - 1, last.T)
    chunk_copy(chunks - 1).start()

    def finish(chunk, carry):
        chunk_copy(chunk).wait()
        return carry

    lax.fori_loop(0, chunks, finish, 0)


def gather_points(picks, x):
    rows, points = x.shape
    blocks = points // LANES
    pieces = points // QUARTERS // 1024
    vmem = pltpu.VMEM
    return pl.pallas_call(
        gather_kernel,
        out_shape=jax.ShapeDtypeStruct((blocks, rows, LANES), jnp.float32),
        in_specs=[pl.BlockSpec(memory_space=pl.ANY)] * 2,
        out_specs=pl.BlockSpec(memory_space=pl.ANY),
        scratch_shapes=[
            vmem((blocks, LANES), jnp.int32),
            vmem((rows, points), jnp.float32),
            vmem((points // QUARTERS, LANES), jnp.float32),
            vmem((blocks, LANES), jnp.int32),
            vmem((blocks, LANES), jnp.int32),
            pltpu.SMEM((16, LANES), jnp.int32),
            pltpu.SMEM((16, LANES), jnp.int32),
            vmem((blocks, rows, LANES), jnp.float32),
            pltpu.SemaphoreType.DMA((1,)),
            pltpu.SemaphoreType.DMA((2,)),
            pltpu.SemaphoreType.DMA((pieces,)),
            pltpu.SemaphoreType.DMA((4,)),
        ],
        compiler_params=pltpu.CompilerParams(vmem_limit_bytes=58 * 2**20),
        name="gather_points",
    )(picks.reshape(blocks, LANES), x)


def transforms_kernel(points, starts_ref, x_ref, bases_ref, turns_ref, res_ref, own_ref, power_ref):
    half = L // 2
    sample = lax.broadcasted_iota(jnp.int32, (L, LANES), 0)
    stacked = [[], []]
    for w in range(W):
        if 0 < w < W - 1:
            start = starts_ref[w]
            turn = lax.rem(start, L)
            cos_start = turns_ref[0, pl.ds(turn, 1), :]
            sin_start = turns_ref[1, pl.ds(turn, 1), :]
            taper = 0.5 - 0.5 * (turns_ref[0] * cos_start + turns_ref[1] * sin_start)
            late = sample >= start
        else:
            taper = turns_ref[2]
        terms = [[], []]
        for comp in range(3):
            series = x_ref[:, comp * 8 : comp * 8 + 8, :].reshape(2 * L, LANES)
            if w == 0:
                frame = series[0:L]
            elif w == W - 1:
                frame = series[L : 2 * L]
            else:
                frame = jnp.where(late, series[0:L], series[L : 2 * L])
            centred = frame - jnp.sum(frame, axis=0, keepdims=True) * (1.0 / L)
            tapered = centred * taper
            terms[0].append(tapered[0:half] + tapered[half:L])
            terms[1].append(tapered[0:half] - tapered[half:L])
        for odd in (0, 1):
            term = jnp.concatenate(terms[odd], axis=1)
            high = term.astype(jnp.bfloat16)
            low = (term - high.astype(jnp.float32)).astype(jnp.bfloat16)
            stacked[odd].append(jnp.concatenate([high, low, high], axis=0))

    for odd in (0, 1):
        power = jnp.zeros((F // 2, 3 * LANES), jnp.float32)
        for w in range(W):
            result = jnp.dot(
                bases_ref[odd], stacked[odd][w], preferred_element_type=jnp.float32
            )
            res_ref[w, odd] = result
            real, imag = result[0 : F // 2], result[F // 2 : F]
            power += real * real + imag * imag
        for comp in range(3):
            span = slice(comp * LANES, (comp + 1) * LANES)
            power_ref[comp, pl.ds(odd, F // 2, stride=2), :] = power[:, span]

    ones = jnp.ones((16, LANES), jnp.bfloat16)
    shares = []
    for comp in range(3):
        power = power_ref[comp]
        high = power.astype(jnp.bfloat16)
        low = (power - high.astype(jnp.float32)).astype(jnp.bfloat16)
        sums = [
            lax.dot_general(
                ones, term, (((1,), (1,)), ((), ())), preferred_element_type=jnp.float32
            )[0:8]
            for term in (high, low)
        ]
        share = (sums[0] + sums[1]) * (SCALE / points)
        shares += [share[:, 0:LANES], share[:, LANES:F]]
    row = lax.broadcasted_iota(jnp.int32, (8, LANES), 0)
    tiles = []
    for tile in range(3):
        place = lax.rem(row + 8 * tile, len(shares))
        value = shares[0]
        for i in range(1, len(shares)):
            value = jnp.where(place == i, shares[i], value)
        tiles.append(value)
    pattern = jnp.concatenate(tiles, axis=0)
    for first in range(0, own_ref.shape[0], 24):
        own_ref[first : first + 24, :] = pattern


def rows_kernel(res_ref, spectra_ref, out_ref, out_sems):
    rows = 8
    bins = F // 2

    def combine(step, carry):
        first = pl.multiple_of(step * rows, rows)
        for odd in (0, 1):
            totals = [None] * 9
            for w in range(W):
                real = [
                    res_ref[w, odd, pl.ds(first, rows), comp * LANES : (comp + 1) * LANES]
                    for comp in range(3)
                ]
                imag = [
                    res_ref[w, odd, pl.ds(bins + first, rows), comp * LANES : (comp + 1) * LANES]
                    for comp in range(3)
                ]
                terms = [real[c] * real[c] + imag[c] * imag[c] for c in range(3)]
                pairs = ((0, 1), (0, 2), (1, 2))
                terms += [real[i] * real[j] + imag[i] * imag[j] for i, j in pairs]
                terms += [real[i] * imag[j] - imag[i] * real[j] for i, j in pairs]
                totals = [b if a is None else a + b for a, b in zip(totals, terms)]
            for row in range(9):
                out_ref[row, pl.ds(2 * first + odd, rows, stride=2), :] = totals[row] * SCALE
        return carry

    pieces = out_sems.shape[0]
    copies = []
    for piece in range(pieces):
        steps = bins // rows // pieces
        lax.fori_loop(piece * steps, (piece + 1) * steps, combine, 0)
        span = pl.ds(piece * (F // pieces), F // pieces)
        copies.append(
            pltpu.make_async_copy(out_ref.at[:, span], spectra_ref.at[:, span], out_sems.at[piece])
        )
        copies[piece].start()
    for copy in copies:
        copy.wait()


def window_transforms(starts, arrived, points, copies):
    vmem = pl.BlockSpec(memory_space=pltpu.VMEM)
    return pl.pallas_call(
        functools.partial(transforms_kernel, points),
        out_shape=(
            jax.ShapeDtypeStruct((W, 2, F, 3 * LANES), jnp.float32),
            jax.ShapeDtypeStruct((copies * 3 * F // LANES, LANES), jnp.float32),
        ),
        in_specs=[pl.BlockSpec(memory_space=pltpu.SMEM)] + [vmem] * 3,
        out_specs=(vmem, vmem),
        scratch_shapes=[pltpu.VMEM((3, F, LANES), jnp.float32)],
        compiler_params=pltpu.CompilerParams(vmem_limit_bytes=28 * 2**20),
        name="window_transforms",
    )(starts, arrived, jnp.asarray(BASES), jnp.asarray(TURNS))


def spectra_rows(transforms):
    return pl.pallas_call(
        rows_kernel,
        out_shape=jax.ShapeDtypeStruct((9, F, LANES), jnp.float32),
        in_specs=[pl.BlockSpec(memory_space=pltpu.VMEM)],
        out_specs=pl.BlockSpec(memory_space=pl.ANY),
        scratch_shapes=[
            pltpu.VMEM((9, F, LANES), jnp.float32),
            pltpu.SemaphoreType.DMA((4,)),
        ],
        compiler_params=pltpu.CompilerParams(vmem_limit_bytes=28 * 2**20),
        cost_estimate=pl.CostEstimate(flops=0, bytes_accessed=12 * 2**20, transcendentals=0),
        name="spectra_rows",
    )(transforms)


def on_device(velocity, starts, picks):
    times, comps, points = velocity.shape
    x = jnp.transpose(velocity, (1, 0, 2)).reshape(comps * times, points)
    chosen = gather_points(picks, x)
    arrived = lax.all_to_all(chosen, DEV, 0, 0, tiled=True)
    plane = ("z", "y")
    transforms, copies = window_transforms(starts, arrived, points, lax.axis_size(plane))
    spectra = spectra_rows(transforms)
    copies = copies.reshape(-1, 3, F // LANES, LANES)
    total = jnp.sum(lax.all_to_all(copies, plane, 0, 0, tiled=True), axis=0)
    total = jnp.sum(lax.all_gather(total, "xl"), axis=0)
    return (spectra, total.reshape(3, F))


def solution(mesh):
    fine = Mesh(mesh.devices.reshape(4, 8, 2, 8), ("grp", *DEV))
    return jax.shard_map(
        on_device,
        mesh=fine,
        in_specs=(P(DEV, None, "grp"), P(), P()),
        out_specs=(P(None, None, ("grp", *DEV)), P("grp", None)),
        check_vma=False,
    )
```

```python
import functools

import jax
import jax.numpy as jnp
import ml_dtypes
import numpy as np
from jax import lax
from jax.experimental import pallas as pl
from jax.experimental.pallas import tpu as pltpu
from jax.sharding import Mesh, PartitionSpec as P

L = 512
F = 256
W = 3
LANES = 128
QUARTERS = 4
DEV = ("z", "xl", "y")


def make_tables():
    half = np.arange(L // 2)
    bins = np.arange(F // 2)
    bases = []
    for odd in (0, 1):
        phase = ((2 * bins[:, None] + odd) * half[None, :] % L) * (2.0 * np.pi / L)
        basis = np.concatenate([np.cos(phase), -np.sin(phase)], axis=0)
        high = basis.astype(ml_dtypes.bfloat16)
        low = (basis - high.astype(np.float64)).astype(ml_dtypes.bfloat16)
        bases.append(np.concatenate([high, high, low], axis=1))
    turn = np.arange(L) * (2.0 * np.pi / L)
    taper = 0.5 - 0.5 * np.cos(turn)
    turns = np.stack([np.cos(turn), np.sin(turn), taper]).astype(np.float32)
    turns = np.ascontiguousarray(np.broadcast_to(turns[:, :, None], (3, L, LANES)))
    return np.stack(bases), turns, float(1.0 / (np.sum(taper * taper) * W))


BASES, TURNS, SCALE = make_tables()


def gather_kernel(
    picks_ref, x_ref, out_ref, picks, x, table, index, which, even, odd, out, sems, index_sems, x_sems, out_sems
):
    rows, points = x.shape
    blocks = out.shape[0]
    quarter = points // QUARTERS
    apart = LANES // QUARTERS
    pieces = x_sems.shape[0]
    width = quarter // pieces
    chunks = out_sems.shape[0]
    size = blocks // chunks
    together = even.shape[0]

    picks_copy = pltpu.make_async_copy(picks_ref, picks, sems.at[0])
    picks_copy.start()
    x_copies = []
    for piece in range(pieces):
        span = pl.ds(piece * width * QUARTERS, width * QUARTERS)
        x_copies.append(pltpu.make_async_copy(x_ref.at[:, span], x.at[:, span], x_sems.at[piece]))
        x_copies[piece].start()
    picks_copy.wait()
    source = picks[...] // LANES
    index[...] = source // QUARTERS * LANES + picks[...] % LANES
    which[...] = source % QUARTERS

    def index_copy(slot, first):
        held = (even, odd)[slot]
        return pltpu.make_async_copy(index.at[pl.ds(first, together)], held, index_sems.at[slot])

    index_copy(0, 0).start()
    index_copy(1, together).start()

    pad = jnp.zeros((apart - rows, LANES), jnp.float32)
    for copy in x_copies:
        copy.wait()
    for block in range(quarter // LANES):
        parts = []
        for q in range(QUARTERS):
            start = (block * QUARTERS + q) * LANES
            parts += [x[:, start : start + LANES], pad]
        table[block * LANES : (block + 1) * LANES, :] = jnp.concatenate(parts, axis=0).T

    point_rows = table.reshape(quarter, 1, LANES)
    row = lax.broadcasted_iota(jnp.int32, (8, LANES), 0)

    def pick(held, block):
        tiles = []
        for tile in range(LANES // 8):
            parts = [
                jnp.broadcast_to(point_rows[held[block, tile * 8 + j]], (8, LANES))
                for j in range(8)
            ]
            step = 1
            while len(parts) > 1:
                mask = (row & step) == 0
                parts = [jnp.where(mask, parts[i], parts[i + 1]) for i in range(0, len(parts), 2)]
                step *= 2
            tiles.append(parts[0])
        return jnp.concatenate(tiles, axis=0)

    def keep(block, turned):
        chosen = jnp.broadcast_to(which[pl.ds(block, 1), :], (rows, LANES))
        value = turned[0:rows]
        for q in range(1, QUARTERS):
            part = turned[q * apart : q * apart + rows]
            value = jnp.where(chosen == q, part, value)
        out[block] = value

    def batch(held, first, before):
        for i in range(together):
            picked = pick(held, i)
            keep(jnp.maximum(first + i - 1, 0), before.T)
            before = picked
        return before

    def chunk_copy(chunk):
        span = pl.ds(chunk * size, size)
        return pltpu.make_async_copy(out.at[span], out_ref.at[span], out_sems.at[chunk])

    def chunk_step(chunk, before):
        for slot, held in enumerate((even, odd)):
            first = chunk * size + slot * together
            index_copy(slot, first).wait()
            before = batch(held, first, before)

            @pl.when(chunk < chunks - 1)
            def _():
                index_copy(slot, first + size).start()

            if slot == 0:

                @pl.when(chunk > 0)
                def _():
                    chunk_copy(chunk - 1).start()

        return before

    last = lax.fori_loop(0, chunks, chunk_step, jnp.zeros((LANES, LANES), jnp.float32))
    keep(blocks - 1, last.T)
    chunk_copy(chunks - 1).start()

    def finish(chunk, carry):
        chunk_copy(chunk).wait()
        return carry

    lax.fori_loop(0, chunks, finish, 0)


def gather_points(picks, x):
    rows, points = x.shape
    blocks = points // LANES
    pieces = points // QUARTERS // 1024
    vmem = pltpu.VMEM
    return pl.pallas_call(
        gather_kernel,
        out_shape=jax.ShapeDtypeStruct((blocks, rows, LANES), jnp.float32),
        in_specs=[pl.BlockSpec(memory_space=pl.ANY)] * 2,
        out_specs=pl.BlockSpec(memory_space=pl.ANY),
        scratch_shapes=[
            vmem((blocks, LANES), jnp.int32),
            vmem((rows, points), jnp.float32),
            vmem((points // QUARTERS, LANES), jnp.float32),
            vmem((blocks, LANES), jnp.int32),
            vmem((blocks, LANES), jnp.int32),
            pltpu.SMEM((16, LANES), jnp.int32),
            pltpu.SMEM((16, LANES), jnp.int32),
            vmem((blocks, rows, LANES), jnp.float32),
            pltpu.SemaphoreType.DMA((1,)),
            pltpu.SemaphoreType.DMA((2,)),
            pltpu.SemaphoreType.DMA((pieces,)),
            pltpu.SemaphoreType.DMA((4,)),
        ],
        compiler_params=pltpu.CompilerParams(vmem_limit_bytes=58 * 2**20),
        name="gather_points",
    )(picks.reshape(blocks, LANES), x)


def transforms_kernel(points, starts_ref, x_ref, bases_ref, turns_ref, res_ref, own_ref, power_ref):
    half = L // 2
    sample = lax.broadcasted_iota(jnp.int32, (L, LANES), 0)
    for w in range(W):
        if 0 < w < W - 1:
            start = starts_ref[w]
            turn = lax.rem(start, L)
            cos_start = turns_ref[0, pl.ds(turn, 1), :]
            sin_start = turns_ref[1, pl.ds(turn, 1), :]
            taper = 0.5 - 0.5 * (turns_ref[0] * cos_start + turns_ref[1] * sin_start)
            late = sample >= start
        else:
            taper = turns_ref[2]
        terms = [[], []]
        for comp in range(3):
            series = x_ref[:, comp * 8 : comp * 8 + 8, :].reshape(2 * L, LANES)
            if w == 0:
                frame = series[0:L]
            elif w == W - 1:
                frame = series[L : 2 * L]
            else:
                frame = jnp.where(late, series[0:L], series[L : 2 * L])
            centred = frame - jnp.sum(frame, axis=0, keepdims=True) * (1.0 / L)
            tapered = centred * taper
            terms[0].append(tapered[0:half] + tapered[half:L])
            terms[1].append(tapered[0:half] - tapered[half:L])
        for odd in (0, 1):
            term = jnp.concatenate(terms[odd], axis=1)
            high = term.astype(jnp.bfloat16)
            low = (term - high.astype(jnp.float32)).astype(jnp.bfloat16)
            res_ref[w, odd] = jnp.dot(
                bases_ref[odd],
                jnp.concatenate([high, low, high], axis=0),
                preferred_element_type=jnp.float32,
            )

    for odd in (0, 1):
        power = jnp.zeros((F // 2, 3 * LANES), jnp.float32)
        for w in range(W):
            real, imag = res_ref[w, odd, 0 : F // 2, :], res_ref[w, odd, F // 2 : F, :]
            power += real * real + imag * imag
        for comp in range(3):
            span = slice(comp * LANES, (comp + 1) * LANES)
            power_ref[comp, pl.ds(odd, F // 2, stride=2), :] = power[:, span]

    ones = jnp.ones((16, LANES), jnp.bfloat16)
    shares = []
    for comp in range(3):
        power = power_ref[comp]
        high = power.astype(jnp.bfloat16)
        low = (power - high.astype(jnp.float32)).astype(jnp.bfloat16)
        sums = [
            lax.dot_general(
                ones, term, (((1,), (1,)), ((), ())), preferred_element_type=jnp.float32
            )[0:8]
            for term in (high, low)
        ]
        share = (sums[0] + sums[1]) * (SCALE / points)
        shares += [share[:, 0:LANES], share[:, LANES:F]]
    row = lax.broadcasted_iota(jnp.int32, (8, LANES), 0)
    tiles = []
    for tile in range(3):
        place = lax.rem(row + 8 * tile, len(shares))
        value = shares[0]
        for i in range(1, len(shares)):
            value = jnp.where(place == i, shares[i], value)
        tiles.append(value)
    pattern = jnp.concatenate(tiles, axis=0)
    for first in range(0, own_ref.shape[0], 24):
        own_ref[first : first + 24, :] = pattern


def rows_kernel(res_ref, spectra_ref, out_ref, out_sems):
    rows = 8
    bins = F // 2

    def combine(step, carry):
        first = pl.multiple_of(step * rows, rows)
        for odd in (0, 1):
            totals = [None] * 9
            for w in range(W):
                real = [
                    res_ref[w, odd, pl.ds(first, rows), comp * LANES : (comp + 1) * LANES]
                    for comp in range(3)
                ]
                imag = [
                    res_ref[w, odd, pl.ds(bins + first, rows), comp * LANES : (comp + 1) * LANES]
                    for comp in range(3)
                ]
                terms = [real[c] * real[c] + imag[c] * imag[c] for c in range(3)]
                pairs = ((0, 1), (0, 2), (1, 2))
                terms += [real[i] * real[j] + imag[i] * imag[j] for i, j in pairs]
                terms += [real[i] * imag[j] - imag[i] * real[j] for i, j in pairs]
                totals = [b if a is None else a + b for a, b in zip(totals, terms)]
            for row in range(9):
                out_ref[row, pl.ds(2 * first + odd, rows, stride=2), :] = totals[row] * SCALE
        return carry

    pieces = out_sems.shape[0]
    copies = []
    for piece in range(pieces):
        steps = bins // rows // pieces
        lax.fori_loop(piece * steps, (piece + 1) * steps, combine, 0)
        span = pl.ds(piece * (F // pieces), F // pieces)
        copies.append(
            pltpu.make_async_copy(out_ref.at[:, span], spectra_ref.at[:, span], out_sems.at[piece])
        )
        copies[piece].start()
    for copy in copies:
        copy.wait()


def window_transforms(starts, arrived, points, copies):
    vmem = pl.BlockSpec(memory_space=pltpu.VMEM)
    return pl.pallas_call(
        functools.partial(transforms_kernel, points),
        out_shape=(
            jax.ShapeDtypeStruct((W, 2, F, 3 * LANES), jnp.float32),
            jax.ShapeDtypeStruct((copies * 3 * F // LANES, LANES), jnp.float32),
        ),
        in_specs=[pl.BlockSpec(memory_space=pltpu.SMEM)] + [vmem] * 3,
        out_specs=(vmem, vmem),
        scratch_shapes=[pltpu.VMEM((3, F, LANES), jnp.float32)],
        compiler_params=pltpu.CompilerParams(vmem_limit_bytes=28 * 2**20),
        name="window_transforms",
    )(starts, arrived, jnp.asarray(BASES), jnp.asarray(TURNS))


def spectra_rows(transforms):
    return pl.pallas_call(
        rows_kernel,
        out_shape=jax.ShapeDtypeStruct((9, F, LANES), jnp.float32),
        in_specs=[pl.BlockSpec(memory_space=pltpu.VMEM)],
        out_specs=pl.BlockSpec(memory_space=pl.ANY),
        scratch_shapes=[
            pltpu.VMEM((9, F, LANES), jnp.float32),
            pltpu.SemaphoreType.DMA((4,)),
        ],
        compiler_params=pltpu.CompilerParams(vmem_limit_bytes=28 * 2**20),
        cost_estimate=pl.CostEstimate(flops=0, bytes_accessed=12 * 2**20, transcendentals=0),
        name="spectra_rows",
    )(transforms)


def on_device(velocity, starts, picks):
    times, comps, points = velocity.shape
    x = jnp.transpose(velocity, (1, 0, 2)).reshape(comps * times, points)
    chosen = gather_points(picks, x)
    arrived = lax.all_to_all(chosen, DEV, 0, 0, tiled=True)
    plane = ("z", "y")
    transforms, copies = window_transforms(starts, arrived, points, lax.axis_size(plane))
    spectra = spectra_rows(transforms)
    copies = copies.reshape(-1, 3, F // LANES, LANES)
    total = jnp.sum(lax.all_to_all(copies, plane, 0, 0, tiled=True), axis=0)
    total = jnp.sum(lax.all_gather(total, "xl"), axis=0)
    return (spectra, total.reshape(3, F))


def solution(mesh):
    fine = Mesh(mesh.devices.reshape(4, 8, 2, 8), ("grp", *DEV))
    return jax.shard_map(
        on_device,
        mesh=fine,
        in_specs=(P(DEV, None, "grp"), P(), P()),
        out_specs=(P(None, None, ("grp", *DEV)), P("grp", None)),
        check_vma=False,
    )
```

```python
import functools

import jax
import jax.numpy as jnp
import ml_dtypes
import numpy as np
from jax import lax
from jax.experimental import pallas as pl
from jax.experimental.pallas import tpu as pltpu
from jax.sharding import Mesh, PartitionSpec as P

L = 512
F = 256
W = 3
LANES = 128
QUARTERS = 4
DEV = ("z", "xl", "y")


def make_tables():
    half = np.arange(L // 2)
    bins = np.arange(F // 2)
    bases = []
    for odd in (0, 1):
        phase = ((2 * bins[:, None] + odd) * half[None, :] % L) * (2.0 * np.pi / L)
        basis = np.concatenate([np.cos(phase), -np.sin(phase)], axis=0)
        high = basis.astype(ml_dtypes.bfloat16)
        low = (basis - high.astype(np.float64)).astype(ml_dtypes.bfloat16)
        bases.append(np.concatenate([high, high, low], axis=1))
    turn = np.arange(L) * (2.0 * np.pi / L)
    taper = 0.5 - 0.5 * np.cos(turn)
    turns = np.stack([np.cos(turn), np.sin(turn), taper]).astype(np.float32)
    turns = np.ascontiguousarray(np.broadcast_to(turns[:, :, None], (3, L, LANES)))
    return np.stack(bases), turns, float(1.0 / (np.sum(taper * taper) * W))


BASES, TURNS, SCALE = make_tables()


def gather_kernel(
    picks_ref, x_ref, out_ref, picks, x, table, index, which, even, odd, out, sems, index_sems, x_sems, out_sems
):
    rows, points = x.shape
    blocks = out.shape[0]
    quarter = points // QUARTERS
    apart = LANES // QUARTERS
    pieces = x_sems.shape[0]
    width = quarter // pieces
    chunks = out_sems.shape[0] // 2
    size = blocks // chunks
    together = even.shape[0]

    x_copies = []
    for piece in range(pieces):
        span = pl.ds(piece * width * QUARTERS, width * QUARTERS)
        x_copies.append(pltpu.make_async_copy(x_ref.at[:, span], x.at[:, span], x_sems.at[piece]))
        x_copies[piece].start()
    picks_copy = pltpu.make_async_copy(picks_ref, picks, sems.at[0])
    picks_copy.start()
    picks_copy.wait()
    source = picks[...] // LANES
    index[...] = source // QUARTERS * LANES + picks[...] % LANES
    which[...] = source % QUARTERS

    def index_copy(slot, first):
        held = (even, odd)[slot]
        return pltpu.make_async_copy(index.at[pl.ds(first, together)], held, index_sems.at[slot])

    index_copy(0, 0).start()
    index_copy(1, together).start()

    pad = jnp.zeros((apart - rows, LANES), jnp.float32)
    for copy in x_copies:
        copy.wait()
    for block in range(quarter // LANES):
        parts = []
        for q in range(QUARTERS):
            start = (block * QUARTERS + q) * LANES
            parts += [x[:, start : start + LANES], pad]
        table[block * LANES : (block + 1) * LANES, :] = jnp.concatenate(parts, axis=0).T

    point_rows = table.reshape(quarter, 1, LANES)
    row = lax.broadcasted_iota(jnp.int32, (8, LANES), 0)

    def pick(held, block):
        tiles = []
        for tile in range(LANES // 8):
            parts = [
                jnp.broadcast_to(point_rows[held[block, tile * 8 + j]], (8, LANES))
                for j in range(8)
            ]
            step = 1
            while len(parts) > 1:
                mask = (row & step) == 0
                parts = [jnp.where(mask, parts[i], parts[i + 1]) for i in range(0, len(parts), 2)]
                step *= 2
            tiles.append(parts[0])
        return jnp.concatenate(tiles, axis=0)

    def keep(block, turned):
        chosen = jnp.broadcast_to(which[pl.ds(block, 1), :], (rows, LANES))
        value = turned[0:rows]
        for q in range(1, QUARTERS):
            part = turned[q * apart : q * apart + rows]
            value = jnp.where(chosen == q, part, value)
        out[block] = value

    def batch(held, first, before):
        for i in range(together):
            picked = pick(held, i)
            keep(jnp.maximum(first + i - 1, 0), before.T)
            before = picked
        return before

    def batch_copy(i):
        span = pl.ds(i * together, together)
        return pltpu.make_async_copy(out.at[span], out_ref.at[span], out_sems.at[i])

    def chunk_step(chunk, before):
        for slot, held in enumerate((even, odd)):
            first = chunk * size + slot * together
            index_copy(slot, first).wait()
            before = batch(held, first, before)

            @pl.when(chunk < chunks - 1)
            def _():
                index_copy(slot, first + size).start()

            if slot == 0:

                @pl.when(chunk > 0)
                def _():
                    batch_copy(2 * chunk - 1).start()

            else:
                batch_copy(2 * chunk).start()

        return before

    last = lax.fori_loop(0, chunks, chunk_step, jnp.zeros((LANES, LANES), jnp.float32))
    keep(blocks - 1, last.T)
    batch_copy(2 * chunks - 1).start()

    def finish(i, carry):
        batch_copy(i).wait()
        return carry

    lax.fori_loop(0, 2 * chunks, finish, 0)


def gather_points(picks, x):
    rows, points = x.shape
    blocks = points // LANES
    pieces = points // QUARTERS // 1024
    vmem = pltpu.VMEM
    return pl.pallas_call(
        gather_kernel,
        out_shape=jax.ShapeDtypeStruct((blocks, rows, LANES), jnp.float32),
        in_specs=[pl.BlockSpec(memory_space=pl.ANY)] * 2,
        out_specs=pl.BlockSpec(memory_space=pl.ANY),
        scratch_shapes=[
            vmem((blocks, LANES), jnp.int32),
            vmem((rows, points), jnp.float32),
            vmem((points // QUARTERS, LANES), jnp.float32),
            vmem((blocks, LANES), jnp.int32),
            vmem((blocks, LANES), jnp.int32),
            pltpu.SMEM((16, LANES), jnp.int32),
            pltpu.SMEM((16, LANES), jnp.int32),
            vmem((blocks, rows, LANES), jnp.float32),
            pltpu.SemaphoreType.DMA((1,)),
            pltpu.SemaphoreType.DMA((2,)),
            pltpu.SemaphoreType.DMA((pieces,)),
            pltpu.SemaphoreType.DMA((8,)),
        ],
        compiler_params=pltpu.CompilerParams(vmem_limit_bytes=58 * 2**20),
        name="gather_points",
    )(picks.reshape(blocks, LANES), x)


def transforms_kernel(points, starts_ref, x_ref, bases_ref, turns_ref, res_ref, own_ref, power_ref):
    half = L // 2
    sample = lax.broadcasted_iota(jnp.int32, (L, LANES), 0)
    stacked = [[], []]
    for w in range(W):
        if 0 < w < W - 1:
            start = starts_ref[w]
            turn = lax.rem(start, L)
            cos_start = turns_ref[0, pl.ds(turn, 1), :]
            sin_start = turns_ref[1, pl.ds(turn, 1), :]
            taper = 0.5 - 0.5 * (turns_ref[0] * cos_start + turns_ref[1] * sin_start)
            late = sample >= start
        else:
            taper = turns_ref[2]
        terms = [[], []]
        for comp in range(3):
            series = x_ref[:, comp * 8 : comp * 8 + 8, :].reshape(2 * L, LANES)
            if w == 0:
                frame = series[0:L]
            elif w == W - 1:
                frame = series[L : 2 * L]
            else:
                frame = jnp.where(late, series[0:L], series[L : 2 * L])
            centred = frame - jnp.sum(frame, axis=0, keepdims=True) * (1.0 / L)
            tapered = centred * taper
            terms[0].append(tapered[0:half] + tapered[half:L])
            terms[1].append(tapered[0:half] - tapered[half:L])
        for odd in (0, 1):
            term = jnp.concatenate(terms[odd], axis=1)
            high = term.astype(jnp.bfloat16)
            low = (term - high.astype(jnp.float32)).astype(jnp.bfloat16)
            stacked[odd].append(jnp.concatenate([high, low, high], axis=0))

    for odd in (0, 1):
        power = jnp.zeros((F // 2, 3 * LANES), jnp.float32)
        for w in range(W):
            result = jnp.dot(
                bases_ref[odd], stacked[odd][w], preferred_element_type=jnp.float32
            )
            res_ref[w, odd] = result
            real, imag = result[0 : F // 2], result[F // 2 : F]
            power += real * real + imag * imag
        for comp in range(3):
            span = slice(comp * LANES, (comp + 1) * LANES)
            power_ref[comp, pl.ds(odd, F // 2, stride=2), :] = power[:, span]

    ones = jnp.ones((16, LANES), jnp.bfloat16)
    shares = []
    for comp in range(3):
        power = power_ref[comp]
        high = power.astype(jnp.bfloat16)
        low = (power - high.astype(jnp.float32)).astype(jnp.bfloat16)
        sums = [
            lax.dot_general(
                ones, term, (((1,), (1,)), ((), ())), preferred_element_type=jnp.float32
            )[0:8]
            for term in (high, low)
        ]
        share = (sums[0] + sums[1]) * (SCALE / points)
        shares += [share[:, 0:LANES], share[:, LANES:F]]
    row = lax.broadcasted_iota(jnp.int32, (8, LANES), 0)
    tiles = []
    for tile in range(3):
        place = lax.rem(row + 8 * tile, len(shares))
        value = shares[0]
        for i in range(1, len(shares)):
            value = jnp.where(place == i, shares[i], value)
        tiles.append(value)
    pattern = jnp.concatenate(tiles, axis=0)
    for first in range(0, own_ref.shape[0], 24):
        own_ref[first : first + 24, :] = pattern


def rows_kernel(res_ref, spectra_ref, out_ref, out_sems):
    rows = 8
    bins = F // 2

    def combine(step, carry):
        first = pl.multiple_of(step * rows, rows)
        for odd in (0, 1):
            totals = [None] * 9
            for w in range(W):
                real = [
                    res_ref[w, odd, pl.ds(first, rows), comp * LANES : (comp + 1) * LANES]
                    for comp in range(3)
                ]
                imag = [
                    res_ref[w, odd, pl.ds(bins + first, rows), comp * LANES : (comp + 1) * LANES]
                    for comp in range(3)
                ]
                terms = [real[c] * real[c] + imag[c] * imag[c] for c in range(3)]
                pairs = ((0, 1), (0, 2), (1, 2))
                terms += [real[i] * real[j] + imag[i] * imag[j] for i, j in pairs]
                terms += [real[i] * imag[j] - imag[i] * real[j] for i, j in pairs]
                totals = [b if a is None else a + b for a, b in zip(totals, terms)]
            for row in range(9):
                out_ref[row, pl.ds(2 * first + odd, rows, stride=2), :] = totals[row] * SCALE
        return carry

    pieces = out_sems.shape[0]
    copies = []
    for piece in range(pieces):
        steps = bins // rows // pieces
        lax.fori_loop(piece * steps, (piece + 1) * steps, combine, 0)
        span = pl.ds(piece * (F // pieces), F // pieces)
        copies.append(
            pltpu.make_async_copy(out_ref.at[:, span], spectra_ref.at[:, span], out_sems.at[piece])
        )
        copies[piece].start()
    for copy in copies:
        copy.wait()


def window_transforms(starts, arrived, points, copies):
    vmem = pl.BlockSpec(memory_space=pltpu.VMEM)
    return pl.pallas_call(
        functools.partial(transforms_kernel, points),
        out_shape=(
            jax.ShapeDtypeStruct((W, 2, F, 3 * LANES), jnp.float32),
            jax.ShapeDtypeStruct((copies * 3 * F // LANES, LANES), jnp.float32),
        ),
        in_specs=[pl.BlockSpec(memory_space=pltpu.SMEM)] + [vmem] * 3,
        out_specs=(vmem, vmem),
        scratch_shapes=[pltpu.VMEM((3, F, LANES), jnp.float32)],
        compiler_params=pltpu.CompilerParams(vmem_limit_bytes=28 * 2**20),
        name="window_transforms",
    )(starts, arrived, jnp.asarray(BASES), jnp.asarray(TURNS))


def spectra_rows(transforms):
    return pl.pallas_call(
        rows_kernel,
        out_shape=jax.ShapeDtypeStruct((9, F, LANES), jnp.float32),
        in_specs=[pl.BlockSpec(memory_space=pltpu.VMEM)],
        out_specs=pl.BlockSpec(memory_space=pl.ANY),
        scratch_shapes=[
            pltpu.VMEM((9, F, LANES), jnp.float32),
            pltpu.SemaphoreType.DMA((4,)),
        ],
        compiler_params=pltpu.CompilerParams(vmem_limit_bytes=28 * 2**20),
        cost_estimate=pl.CostEstimate(flops=0, bytes_accessed=12 * 2**20, transcendentals=0),
        name="spectra_rows",
    )(transforms)


def on_device(velocity, starts, picks):
    times, comps, points = velocity.shape
    x = jnp.transpose(velocity, (1, 0, 2)).reshape(comps * times, points)
    chosen = gather_points(picks, x)
    arrived = lax.all_to_all(chosen, DEV, 0, 0, tiled=True)
    plane = ("z", "y")
    transforms, copies = window_transforms(starts, arrived, points, lax.axis_size(plane))
    spectra = spectra_rows(transforms)
    copies = copies.reshape(-1, 3, F // LANES, LANES)
    total = jnp.sum(lax.all_to_all(copies, plane, 0, 0, tiled=True), axis=0)
    total = jnp.sum(lax.all_gather(total, "xl"), axis=0)
    return (spectra, total.reshape(3, F))


def solution(mesh):
    fine = Mesh(mesh.devices.reshape(4, 8, 2, 8), ("grp", *DEV))
    return jax.shard_map(
        on_device,
        mesh=fine,
        in_specs=(P(DEV, None, "grp"), P(), P()),
        out_specs=(P(None, None, ("grp", *DEV)), P("grp", None)),
        check_vma=False,
    )
```
